256 devices in a mesh: row: 16 (over z_lo, x, core), col: 16 (over y, z_hi).
Axes of the slice: x: 4, y: 4, z: 8 (z_hi: 4, z_lo: 2; z = z_hi * 2 + z_lo), core: 2. Of those that a mesh axis runs over, the one named last changes fastest.
Arguments:
- tokens: bfloat16 [1024, 8192], P('col', 'row'), may hold values from -6 to 6
- gate_pre: bfloat16 [1024, 28672], P('row', 'col'), may hold values from -10 to 10
- up_pre: bfloat16 [1024, 28672], P('row', 'col'), may hold values from -6 to 6
- grad_out: bfloat16 [1024, 8192], P('col', 'row'), may hold values from -6 to 6
- gate_weight: bfloat16 [8192, 28672], P('row', 'col'), may hold values from -0.0625 to 0.0625
- up_weight: bfloat16 [8192, 28672], P('row', 'col'), may hold values from -0.0625 to 0.0625
- down_weight: bfloat16 [28672, 8192], P('col', 'row'), may hold values from -0.03125 to 0.03125
Outputs:
- grad_tokens: bfloat16 [1024, 8192], P('col', 'row')
- grad_gate: bfloat16 [8192, 28672], P('row', 'col')
- grad_up: bfloat16 [8192, 28672], P('row', 'col')
- grad_down: bfloat16 [28672, 8192], P('col', 'row')
The draws below stay inside these ranges and needn't reach their ends.
All inputs are finite; a program needn't handle non-finite values.
Results may differ from the reference program's by a relative error of at most 0.005.
Values may be sent and summed in bfloat16 or wider, within the bound.
A program may use at most 128 MiB of HBM per device.

```python
import jax
import jax.numpy as jnp
from jax import lax

D = 8192
FF = 28672
TOKENS = 1024


def levels(stream_key, dims, cuts, least, high):
    def one(axis_at, blocks):
        draws = jax.random.uniform(jax.random.fold_in(jax.random.fold_in(stream_key, 6), axis_at), (blocks,), jnp.float32, least / len(cuts), high / len(cuts))
        return jnp.repeat(jnp.exp(draws), dims[axis_at] // blocks).reshape((-1,) + (1,) * (len(dims) - axis_at - 1))

    loudness = one(*cuts[0])
    for cut in cuts[1:]:
        loudness = loudness * one(*cut)
    return loudness


def centred(rng, shape, deviation, most, pieces=(), kind=jnp.bfloat16):
    drawn = jax.random.normal(rng, shape, jnp.float32) * deviation
    if len(pieces) > 0:
        drawn = levels(rng, shape, pieces, -0.22, 0.18) * drawn
    return jnp.clip(drawn, min=-most, max=most).astype(kind)


def setup_inputs(seed: int = 0) -> dict:
    key_of = jax.random.split(jax.random.key(seed), 8)
    return {
        "tokens": centred(key_of[0], (TOKENS, D), 1.0, 6.0, ((0, 16), (1, 16))),
        "gate_pre": centred(key_of[1], (TOKENS, FF), 2.0, 10.0, ((0, 16), (1, 16))),
        "up_pre": centred(key_of[2], (TOKENS, FF), 1.0, 6.0, ((0, 16), (1, 16))),
        "grad_out": centred(key_of[3], (TOKENS, D), 1.0, 6.0, ((0, 16), (1, 16))),
        "gate_weight": centred(key_of[4], (D, FF), D ** -0.5, 0.0625, ((0, 16), (1, 16))),
        "up_weight": centred(key_of[5], (D, FF), D ** -0.5, 0.0625, ((0, 16), (1, 16))),
        "down_weight": centred(key_of[6], (FF, D), FF ** -0.5, 0.03125, ((0, 16), (1, 16))),
    }


def reference(tokens, gate_pre, up_pre, grad_out, gate_weight, up_weight, down_weight):
    hidden_grad = lax.dot_general(grad_out, down_weight, (((1,), (1,)), ((), ())), preferred_element_type=jnp.float32)
    gate_raw = gate_pre.astype(jnp.float32)
    up_raw = up_pre.astype(jnp.float32)
    sigmoid_gate = jax.nn.sigmoid(gate_raw)
    hidden = (gate_raw * sigmoid_gate * up_raw).astype(jnp.bfloat16)
    gate_grad = (hidden_grad * up_raw * sigmoid_gate * (1.0 + gate_raw * (1.0 - sigmoid_gate))).astype(jnp.bfloat16)
    up_grad = (hidden_grad * gate_raw * sigmoid_gate).astype(jnp.bfloat16)
    contract_last = (((1,), (1,)), ((), ()))
    grad_tokens = lax.dot_general(gate_grad, gate_weight, contract_last, preferred_element_type=jnp.float32)
    grad_tokens = grad_tokens + lax.dot_general(up_grad, up_weight, contract_last, preferred_element_type=jnp.float32)
    contract_first = (((0,), (0,)), ((), ()))
    grad_gate = lax.dot_general(tokens, gate_grad, contract_first, preferred_element_type=jnp.float32)
    grad_up = lax.dot_general(tokens, up_grad, contract_first, preferred_element_type=jnp.float32)
    grad_down = lax.dot_general(hidden, grad_out, contract_first, preferred_element_type=jnp.float32)
    return (grad_tokens.astype(jnp.bfloat16), grad_gate.astype(jnp.bfloat16), grad_up.astype(jnp.bfloat16), grad_down.astype(jnp.bfloat16))
```

```python
import jax
import jax.numpy as jnp
from jax import lax
from jax.experimental import pallas as pl
from jax.experimental.pallas import tpu as pltpu
from jax.sharding import PartitionSpec as P

MESH = pl.DeviceIdType.MESH
F32 = jnp.float32
BF16 = jnp.bfloat16

NT = (((1,), (1,)), ((), ()))
TN = (((0,), (0,)), ((), ()))

TOK = 1024
FEAT = 512
HID = 1792
HALF = HID // 2
CHUNK = 256
QUART = 64
ORDER = (2, 1, 3, 0)
N_COPY = 128


def dot(a, b, dims):
    return lax.dot_general(a, b, dims, preferred_element_type=F32)


def kernel(
    tok_in, gate_in, up_in, go_in, wg_in, wu_in, wd_in,
    gt_out, gg_out, gu_out, gd_out,
    wg, wu, wd, tok, go, gate, up, hid, ggrad, ugrad, hg,
    keep, sib_send, sib_recv, x_send, x_recv, acc, z_send, z_recv,
    d_send, d_recv, d_sum, h_send, h_recv,
    send_sem, recv_sem, local_sem,
):
    row = lax.axis_index("row")
    col = lax.axis_index("col")
    zl, x, k = row // 8, (row // 2) % 4, row % 2
    y, zh = col // 4, col % 4
    chip = zl * 4 + x

    def dev(dzl=0, dx=0, dk=0, dy=0, dzh=0):
        return (
            ((zl + dzl) % 2) * 8 + ((x + dx) % 4) * 2 + (k + dk) % 2,
            ((y + dy) % 4) * 4 + (zh + dzh) % 4,
        )

    copies = []

    def send(src, dst, **offset):
        i = len(copies)
        cp = pltpu.make_async_remote_copy(
            src_ref=src, dst_ref=dst, send_sem=send_sem.at[i], recv_sem=recv_sem.at[i],
            device_id=dev(**offset), device_id_type=MESH,
        )
        cp.start()
        copies.append(cp)
        return cp

    locals_ = []

    def load(src, dst):
        cp = pltpu.make_async_copy(src, dst, local_sem.at[len(locals_)])
        cp.start()
        locals_.append(cp)
        return cp

    l_go = load(go_in, go.at[y, zh])
    l_gate = load(gate_in, gate.at[chip, k])
    l_up = load(up_in, up.at[chip, k])
    l_wd = load(wd_in, wd)
    l_tok = load(tok_in, tok.at[y, zh])
    l_wg = load(wg_in, wg)
    l_wu = load(wu_in, wu)

    peers = (
        [dict(dk=1), dict(dzl=1)]
        + [dict(dx=d) for d in (1, 2, 3)]
        + [dict(dy=d) for d in (1, 2, 3)]
        + [dict(dzh=d) for d in (1, 2, 3)]
    )
    barrier = pltpu.get_barrier_semaphore()
    for p in peers:
        pl.semaphore_signal(barrier, inc=1, device_id=dev(**p), device_id_type=MESH)
    pl.semaphore_wait(barrier, len(peers))

    c_go_h = [send(go_in, go.at[y, zh], dzh=d) for d in (1, 2, 3)]
    c_g_x = [send(gate_in, gate.at[chip, k], dx=d) for d in (1, 2, 3)]
    c_u_z = send(up_in, up.at[chip, k], dzl=1)
    c_u_x = [send(up_in, up.at[chip, k], dx=d) for d in (1, 2, 3)]
    c_g_z = [send(gate_in, gate.at[chip, k], dzl=1)]
    c_tok_h = [send(tok_in, tok.at[y, zh], dzh=d) for d in (1, 2, 3)]

    l_go.wait()
    for c in c_go_h:
        c.wait_recv()
    c_go_y = {d: send(go.at[y], go.at[y], dy=d) for d in (2, 1, 3)}

    other = (1 - zl) * 4 + x
    c_u_z.wait_recv()
    c_u_x2 = [send(up.at[other, k], up.at[other, k], dx=d) for d in (1, 2, 3)]

    l_tok.wait()
    for c in c_tok_h:
        c.wait_recv()
    c_tok_y = {d: send(tok.at[y], tok.at[y], dy=d) for d in (2, 1, 3)}

    for d, c in zip((1, 2, 3), c_g_x):
        c.wait_recv()
        at = zl * 4 + (x + 4 - d) % 4
        c_g_z.append(send(gate.at[at, k], gate.at[at, k], dzl=1))

    l_wd.wait()
    mine = pl.ds(pl.multiple_of(k * HALF, 128), HALF)
    theirs = pl.ds(pl.multiple_of((1 - k) * HALF, 128), HALF)
    own = pl.ds(pl.multiple_of(x * QUART, QUART), QUART)
    st = [dict() for _ in ORDER]

    def plane(j):
        return (y + ORDER[j]) % 4

    def s0(j):
        if ORDER[j]:
            c_go_y[4 - ORDER[j]].wait_recv()
        a = go[plane(j)].reshape(CHUNK, FEAT)
        sib_send[j] = dot(a, wd[theirs, :], NT)
        st[j]["sib"] = send(sib_send.at[j], sib_recv.at[j], dk=1)
        keep[j] = dot(a, wd[mine, :], NT)

    def s1(j):
        st[j]["sib"].wait_recv()

        @pl.loop(0, CHUNK // 16)
        def _(i):
            r = pl.ds(pl.multiple_of(i * 16, 16), 16)
            x_send[j, r] = (keep[j, r] + sib_recv[j, r]).astype(BF16)

        st[j]["x"] = []
        for d in (2, 1, 3):
            r = pl.ds(pl.multiple_of((x + d) % 4 * QUART, QUART), QUART)
            st[j]["x"].append(send(x_send.at[j, r], x_recv.at[j, d - 1], dx=d))

    def s2(j):
        for c in st[j]["x"]:
            c.wait_recv()

        @pl.loop(0, QUART // 16)
        def _(i):
            r = pl.ds(pl.multiple_of(i * 16, 16), 16)
            o = pl.ds(pl.multiple_of(x * QUART + i * 16, 16), 16)
            t = keep[j, o] + sib_recv[j, o]
            for d in range(3):
                t = t + x_recv[j, d, r].astype(F32)
            acc[j, r] = t
            z_send[j, r] = t.astype(BF16)

        st[j]["z"] = send(z_send.at[j], z_recv.at[j], dzl=1)

    def s3(j):
        st[j]["z"].wait_recv()
        p = plane(j)

        @pl.loop(0, QUART // 16)
        def _(i):
            r = pl.ds(pl.multiple_of(i * 16, 16), 16)
            o = pl.ds(pl.multiple_of(x * QUART + i * 16, 16), 16)
            hg[k, p, o] = (acc[j, r] + z_recv[j, r].astype(F32)).astype(BF16)

        q = hg.at[k, p, own]
        st[j]["ag"] = [send(q, q, dx=d) for d in (2, 1, 3)]

    def s4(j):
        for c in st[j]["ag"]:
            c.wait_recv()
        q = hg.at[k, plane(j)]
        st[j]["sag"] = send(q, q, dk=1)

    def s5(j):
        st[j]["sag"].wait_recv()
        p = plane(j)
        for b in range(4):
            ch, kk = 2 * p + b // 2, b % 2

            @pl.loop(0, 8)
            def _(i):
                r = pl.ds(pl.multiple_of(i // 2 * 16, 16), 16)
                o = pl.ds(pl.multiple_of(b * 64 + i // 2 * 16, 16), 16)
                h = i % 2
                c = pl.ds(pl.multiple_of(h * HALF, 128), HALF)
                g = gate[ch, kk, r, c].astype(F32)
                u = up[ch, kk, r, c].astype(F32)
                t = hg[h, p, o].astype(F32)
                s = 1.0 / (1.0 + jnp.exp(-g))
                ts = t * s
                ggrad[p, o, c] = (ts * u * (1.0 + g * (1.0 - s))).astype(BF16)
                ugrad[p, o, c] = (ts * g).astype(BF16)

        part = dot(ggrad[p], wg[...], NT) + dot(ugrad[p], wu[...], NT)
        if ORDER[j]:
            d_send[ORDER[j] - 1] = part
            st[j]["d"] = send(d_send.at[ORDER[j] - 1], d_recv.at[ORDER[j] - 1], dy=ORDER[j])
        else:
            d_sum[...] = part

    s0(0)
    s0(1)
    s1(0)
    s0(2)
    s1(1)
    s0(3)
    s1(2)
    s1(3)

    for c in c_g_z:
        c.wait_recv()
    for c in c_u_x + c_u_x2:
        c.wait_recv()
    l_gate.wait()
    l_up.wait()
    c_g_s = send(gate.at[:, k], gate.at[:, k], dk=1)
    c_u_s = send(up.at[:, k], up.at[:, k], dk=1)

    s2(0)
    s3(0)
    s2(1)
    s3(1)

    c_g_s.wait_recv()
    c_u_s.wait_recv()

    @pl.loop(0, 64)
    def _(i):
        r = pl.ds(pl.multiple_of(i % 4 * 16, 16), 16)
        b = i // 4
        o = pl.ds(pl.multiple_of(b % 4 * 64 + i % 4 * 16, 16), 16)
        g = gate[b // 2, b % 2, r].astype(F32)
        u = up[b // 2, b % 2, r].astype(F32)
        hid[b // 4, o] = (g * u * (1.0 / (1.0 + jnp.exp(-g)))).astype(BF16)

    l_wg.wait()
    l_wu.wait()
    s4(0)
    s2(2)
    s3(2)
    s5(0)
    s4(1)
    s2(3)
    s3(3)
    s5(1)

    def grad_down():
        b = go[...].reshape(TOK, FEAT)

        @pl.loop(0, 7)
        def _(i):
            c = pl.ds(pl.multiple_of(i * 256, 256), 256)
            a = hid[:, :, c].reshape(TOK, 256)
            gd_out[c, :] = dot(a, b, TN).astype(BF16)

    grad_down()
    s4(2)
    s5(2)
    s4(3)
    s5(3)

    for j in range(3):
        st[j]["d"].wait_recv()
    tot = d_sum[...] + d_recv[0] + d_recv[1] + d_recv[2]
    d_sum[...] = tot
    h_send[...] = tot.astype(BF16)
    c_h = []
    for d in (2, 1, 3):
        r = pl.ds(pl.multiple_of((zh + d) % 4 * 64, 64), 64)
        c_h.append(send(h_send.at[r], h_recv.at[d - 1], dzh=d))

    for d in (1, 2, 3):
        c_tok_y[d].wait_recv()
    a = tok[...].reshape(TOK, FEAT)

    @pl.loop(0, 7)
    def _(i):
        c = pl.ds(pl.multiple_of(i * 256, 256), 256)
        gg_out[:, c] = dot(a, ggrad[:, :, c].reshape(TOK, 256), TN).astype(BF16)
        gu_out[:, c] = dot(a, ugrad[:, :, c].reshape(TOK, 256), TN).astype(BF16)

    for c in c_h:
        c.wait_recv()
    t = d_sum[pl.ds(pl.multiple_of(zh * 64, 64), 64), :]
    for d in range(3):
        t = t + h_recv[d].astype(F32)
    gt_out[...] = t.astype(BF16)
    for c in copies:
        c.wait_send()


def on_device(tokens, gate_pre, up_pre, grad_out, gate_weight, up_weight, down_weight):
    hbm = pl.BlockSpec(memory_space=pl.ANY)
    vmem = pl.BlockSpec(memory_space=pltpu.VMEM)
    bf = lambda *s: pltpu.VMEM(s, BF16)
    fl = lambda *s: pltpu.VMEM(s, F32)
    return pl.pallas_call(
        kernel,
        out_shape=(
            jax.ShapeDtypeStruct((64, FEAT), BF16),
            jax.ShapeDtypeStruct((FEAT, HID), BF16),
            jax.ShapeDtypeStruct((FEAT, HID), BF16),
            jax.ShapeDtypeStruct((HID, FEAT), BF16),
        ),
        in_specs=[hbm] * 7,
        out_specs=(vmem,) * 4,
        scratch_shapes=[
            bf(FEAT, HID), bf(FEAT, HID), bf(HID, FEAT),
            bf(4, 4, 64, FEAT), bf(4, 4, 64, FEAT),
            bf(8, 2, 64, HID), bf(8, 2, 64, HID),
            bf(4, CHUNK, HID), bf(4, CHUNK, HID), bf(4, CHUNK, HID),
            bf(2, 4, CHUNK, HALF),
            fl(4, CHUNK, HALF), fl(4, CHUNK, HALF), fl(4, CHUNK, HALF),
            bf(4, CHUNK, HALF), bf(4, 3, QUART, HALF),
            fl(4, QUART, HALF), bf(4, QUART, HALF), bf(4, QUART, HALF),
            fl(3, CHUNK, FEAT), fl(3, CHUNK, FEAT), fl(CHUNK, FEAT),
            bf(CHUNK, FEAT), bf(3, 64, FEAT),
            pltpu.SemaphoreType.DMA((N_COPY,)),
            pltpu.SemaphoreType.DMA((N_COPY,)),
            pltpu.SemaphoreType.DMA((8,)),
        ],
        compiler_params=pltpu.CompilerParams(
            collective_id=0, has_side_effects=True, vmem_limit_bytes=62 * 2**20
        ),
        cost_estimate=pl.CostEstimate(
            flops=12 * TOK * FEAT * HID, bytes_accessed=2**24, transcendentals=TOK * HID
        ),
        name="swiglu_backward",
    )(tokens, gate_pre, up_pre, grad_out, gate_weight, up_weight, down_weight)


def solution(mesh):
    in_specs = (
        P("col", "row"),
        P("row", "col"),
        P("row", "col"),
        P("col", "row"),
        P("row", "col"),
        P("row", "col"),
        P("col", "row"),
    )
    out_specs = (P("col", "row"), P("row", "col"), P("row", "col"), P("col", "row"))
    return jax.shard_map(
        on_device, mesh=mesh, in_specs=in_specs, out_specs=out_specs, check_vma=False
    )
```

```python
import jax
import jax.numpy as jnp
from jax import lax
from jax.experimental import pallas as pl
from jax.experimental.pallas import tpu as pltpu
from jax.sharding import PartitionSpec as P

MESH = pl.DeviceIdType.MESH
F32 = jnp.float32
BF16 = jnp.bfloat16

NN = (((1,), (0,)), ((), ()))
TN = (((0,), (0,)), ((), ()))

TOK = 1024
FEAT = 512
HID = 1792
HALF = HID // 2
PLANE = 256
CHUNK = 128
PART = 32
ORDER = ((2, 1), (2, 0), (3, 1), (0, 1), (1, 1), (1, 0), (3, 0), (0, 0))
N_COPY = 192
SCHEDULE = (
    ("turn_down",), ("turn_up",), ("go_y",), ("gate_relay",), ("s0", 3), ("s0", 7), ("up_relay",),
    ("s1", 3), ("s1", 7), ("gate_last",), ("up_other",), ("s0", 0), ("s0", 1), ("s2", 3), ("s1", 0),
    ("s1", 1), ("tok_h",), ("s2", 7), ("s0", 2), ("s0", 4), ("s0", 5), ("s0", 6), ("s1", 2),
    ("s1", 4), ("s1", 5), ("up_other_relay",), ("s1", 6), ("s2", 0), ("s2", 1), ("s2", 2),
    ("s2", 4), ("s3", 3), ("s2", 5), ("gather_core",), ("s2", 6), ("s3", 7), ("tok_y",), ("s3", 0),
    ("s5", 3), ("s3", 1), ("s3", 2), ("core_arrive",), ("hidden",), ("s6", 3), ("s5", 0), ("s3", 4),
    ("grad_down",), ("s5", 1), ("s6", 0), ("s3", 5), ("s6", 1), ("s5", 2), ("s5", 7), ("s3", 6),
    ("s6", 2), ("s5", 4), ("s6", 7), ("s6", 4), ("s5", 5), ("s6", 5), ("s5", 6), ("s6", 6),
    ("s7", 1), ("wg",), ("s7", 0), ("final",),
)


def dot(a, b, dims):
    return lax.dot_general(a, b, dims, preferred_element_type=F32)


def ds(start, size):
    return pl.ds(pl.multiple_of(start, size), size)


def kernel(
    tok_in, gate_in, up_in, go_in, wg_in, wu_in, wd_in,
    gt_out, gg_out, gu_out, gd_out,
    wg, wu, wd, wg_t, wu_t, wd_t, tok, go, gate, up, hid, ggrad, ugrad, hg,
    keep, sib_send, sib_recv, x_send, x_recv, acc, z_send, z_recv,
    d_send, d_recv, d_sum, h_send, h_recv,
    send_sem, recv_sem, local_sem,
):
    row = lax.axis_index("row")
    col = lax.axis_index("col")
    zl, x, k = row // 8, (row // 2) % 4, row % 2
    y, zh = col // 4, col % 4
    chip = zl * 4 + x

    def dev(dzl=0, dx=0, dk=0, dy=0, dzh=0):
        return (
            ((zl + dzl) % 2) * 8 + ((x + dx) % 4) * 2 + (k + dk) % 2,
            ((y + dy) % 4) * 4 + (zh + dzh) % 4,
        )

    copies = []

    def prepare(src, dst, **offset):
        i = len(copies)
        cp = pltpu.make_async_remote_copy(
            src_ref=src, dst_ref=dst, send_sem=send_sem.at[i], recv_sem=recv_sem.at[i],
            device_id=dev(**offset), device_id_type=MESH,
        )
        copies.append(cp)
        return cp

    def send(src, dst, **offset):
        cp = prepare(src, dst, **offset)
        cp.start()
        return cp

    def arrive(group):
        for c in group:
            c.wait_recv()

    def both_ways(q):
        return send(q, q, dx=1), send(q, q, dx=3)

    def relay(pair, q_left, q_right, rows):
        pair[0].wait_recv()
        q = q_left(slice(0, rows // 2))
        to_right = send(q, q, dx=1)
        pair[1].wait_recv()
        q = q_right(slice(rows // 2, rows))
        return to_right, send(q, q, dx=3)

    locals_ = []

    def load(src, dst):
        cp = pltpu.make_async_copy(src, dst, local_sem.at[len(locals_)])
        cp.start()
        locals_.append(cp)
        return cp

    l_go = load(go_in, go.at[y, zh])
    l_wd = load(wd_in, wd)
    l_gate = load(gate_in, gate.at[chip, k])
    l_up = load(up_in, up.at[chip, k])
    l_tok = load(tok_in, tok.at[y, zh])
    l_wg = load(wg_in, wg)
    l_wu = load(wu_in, wu)

    peers = (
        [dict(dk=1), dict(dzl=1)]
        + [dict(dx=d) for d in (1, 2, 3)]
        + [dict(dy=d) for d in (1, 2, 3)]
        + [dict(dzh=d) for d in (1, 2, 3)]
    )
    barrier = pltpu.get_barrier_semaphore()
    for p in peers:
        pl.semaphore_signal(barrier, inc=1, device_id=dev(**p), device_id_type=MESH)
    pl.semaphore_wait(barrier, len(peers))

    other = (1 - zl) * 4 + x
    left, right, across = (zl * 4 + (x + d) % 4 for d in (3, 1, 2))
    o_left, o_right = ((1 - zl) * 4 + (x + d) % 4 for d in (3, 1))
    mine = ds(k * HALF, HALF)
    theirs = ds((1 - k) * HALF, HALF)
    st = [dict() for _ in ORDER]
    got = {}
    planes = set()

    def plane(j):
        return (y + ORDER[j][0]) % 4

    def rows(j, start, size):
        return ds(ORDER[j][1] * CHUNK + start, size)

    def s0(j):
        dy, half = ORDER[j]
        if dy and dy not in planes:
            planes.add(dy)
            got["go_y"][4 - dy].wait_recv()
        a = go[plane(j), 2 * half : 2 * half + 2].reshape(CHUNK, FEAT)
        sib_send[j] = dot(a, wd_t[:, theirs], NN)
        st[j]["sib"] = send(sib_send.at[j], sib_recv.at[j], dk=1)
        keep[j] = dot(a, wd_t[:, mine], NN)

    def s1(j):
        st[j]["sib"].wait_recv()

        @pl.loop(0, CHUNK // 16)
        def _(i):
            r = ds(i * 16, 16)
            x_send[j, r] = (keep[j, r] + sib_recv[j, r]).astype(BF16)

        st[j]["x"] = []
        for d in (2, 1, 3):
            r = ds((x + d) % 4 * PART, PART)
            st[j]["x"].append(send(x_send.at[j, r], x_recv.at[j, d - 1], dx=d))

    def s2(j):
        arrive(st[j]["x"])
        for i in range(PART // 16):
            r = pl.ds(i * 16, 16)
            o = ds(x * PART + i * 16, 16)
            t = keep[j, o] + sib_recv[j, o]
            for d in range(3):
                t = t + x_recv[j, d, r].astype(F32)
            acc[j, r] = t
            z_send[j, r] = t.astype(BF16)
        st[j]["z"] = send(z_send.at[j], z_recv.at[j], dzl=1)

    def s3(j):
        st[j]["z"].wait_recv()
        p = plane(j)
        for i in range(PART // 16):
            r = pl.ds(i * 16, 16)
            hg[k, p, rows(j, x * PART + i * 16, 16)] = (
                acc[j, r] + z_recv[j, r].astype(F32)
            ).astype(BF16)
        q = hg.at[k, p, rows(j, x * PART, PART)]
        st[j]["ar"] = [send(q, q, dx=d) for d in (2, 1, 3)]

    def s5(j):
        arrive(st[j]["ar"])
        q = hg.at[k, plane(j), rows(j, 0, CHUNK)]
        st[j]["core"] = send(q, q, dk=1)

    def s6(j):
        st[j]["core"].wait_recv()
        p = plane(j)
        dy, half = ORDER[j]
        for b in range(2):

            @pl.loop(0, 8, unroll=4)
            def _(i):
                r = ds(i // 2 * 16, 16)
                o = rows(j, b * 64 + i // 2 * 16, 16)
                h = i % 2
                c = ds(h * HALF, HALF)
                g = gate[2 * p + half, b, r, c].astype(F32)
                u = up[2 * p + half, b, r, c].astype(F32)
                t = hg[h, p, o].astype(F32)
                s = 1.0 / (1.0 + jnp.exp(-g))
                ts = t * s
                ggrad[p, o, c] = (ts * u * (1.0 + g * (1.0 - s))).astype(BF16)
                ugrad[p, o, c] = (ts * g).astype(BF16)

        o = rows(j, 0, CHUNK)
        part = dot(ggrad[p, o], wg_t[...], NN) + dot(ugrad[p, o], wu_t[...], NN)
        if dy:
            d_send[dy - 1, o] = part.astype(BF16)
            st[j]["d"] = send(d_send.at[dy - 1, o], d_recv.at[dy - 1, o], dy=dy)
        else:
            d_sum[o] = part

    def s7(half):
        for j, (dy, h) in enumerate(ORDER):
            if dy and h == half:
                st[j]["d"].wait_recv()
        o = pl.ds(half * CHUNK, CHUNK)
        t = d_sum[o]
        for d in range(3):
            t = t + d_recv[d, o].astype(F32)
        d_sum[o] = t
        h_send[o] = t.astype(BF16)
        for d, c in got["h"].items():

            @pl.when((zh + d) % 4 // 2 == half)
            def _():
                c.start()

    def hidden():
        @pl.loop(0, 64, unroll=4)
        def _(i):
            r = ds(i % 4 * 16, 16)
            b = i // 4
            o = ds(b % 4 * 64 + i % 4 * 16, 16)
            g = gate[b // 2, b % 2, r].astype(F32)
            u = up[b // 2, b % 2, r].astype(F32)
            hid[b // 4, o] = (g * u * (1.0 / (1.0 + jnp.exp(-g)))).astype(BF16)

    def grad_down():
        a, b = hid[...].reshape(TOK, HID), go[...].reshape(TOK, FEAT)
        gd_out[...] = dot(a, b, TN).astype(BF16)

    def tok_h():
        got["tok_h"] = [send(tok_in, tok.at[y, zh], dzh=d) for d in (2, 1, 3)]

    def tok_y():
        l_tok.wait()
        arrive(got["tok_h"])
        got["tok_y"] = [send(tok.at[y], tok.at[y], dy=d) for d in (2, 1, 3)]

    def gate_z(at):
        got["g_z"].append(send(gate.at[at, k], gate.at[at, k], dzl=1))

    def gate_relay():
        got["g_r"] = relay(
            got["g_x"], lambda r: gate.at[left, k, r], lambda r: gate.at[right, k, r], 64
        )
        gate_z(left)
        gate_z(right)

    def gate_last():
        arrive(got["g_r"])
        gate_z(across)

    def up_relay():
        got["u_r"] = relay(
            got["u_x"], lambda r: up.at[left, k, r], lambda r: up.at[right, k, r], 64
        )

    def up_other():
        got["u_z"].wait_recv()
        got["u_x2"] = both_ways(up.at[other, k])

    def up_other_relay():
        got["u_r2"] = relay(
            got["u_x2"], lambda r: up.at[o_left, k, r], lambda r: up.at[o_right, k, r], 64
        )

    def gather_core():
        arrive(got["g_z"])
        arrive(got["u_r"])
        arrive(got["u_r2"])
        l_gate.wait()
        l_up.wait()
        got["core"] = [
            send(gate.at[:, k], gate.at[:, k], dk=1),
            send(up.at[:, k], up.at[:, k], dk=1),
        ]

    got["h"] = {
        d: prepare(h_send.at[ds((zh + d) % 4 * 64, 64)], h_recv.at[d - 1], dzh=d)
        for d in (2, 1, 3)
    }

    def go_y():
        arrive(go_h)
        l_go.wait()
        got["go_y"] = {d: send(go.at[y], go.at[y], dy=d) for d in (2, 1, 3)}
        got["u_z"] = send(up_in, up.at[chip, k], dzl=1)
        got["g_z"] = [send(gate_in, gate.at[chip, k], dzl=1)]

    def core_arrive():
        arrive(got["core"])

    def turn_down():
        l_wd.wait()
        wd_t[...] = wd[...].T

    def turn_up():
        l_wg.wait()
        l_wu.wait()
        wg_t[...] = wg[...].T
        wu_t[...] = wu[...].T

    def wg_grads():
        arrive(got["tok_y"])
        a = tok[...].reshape(TOK, FEAT)
        gg_out[...] = dot(a, ggrad[...].reshape(TOK, HID), TN).astype(BF16)
        gu_out[...] = dot(a, ugrad[...].reshape(TOK, HID), TN).astype(BF16)

    def final():
        arrive(got["h"].values())
        t = d_sum[ds(zh * 64, 64), :]
        for d in range(3):
            t = t + h_recv[d].astype(F32)
        gt_out[...] = t.astype(BF16)

    go_h = [send(go_in, go.at[y, zh], dzh=d) for d in (2, 1, 3)]
    q = gate.at[chip, k]
    got["g_x"] = send(gate_in, q, dx=1), send(gate_in, q, dx=3)
    q = up.at[chip, k]
    got["u_x"] = send(up_in, q, dx=1), send(up_in, q, dx=3)

    steps = dict(
        turn_down=turn_down,
        turn_up=turn_up,
        go_y=go_y,
        gate_relay=gate_relay,
        s0=s0,
        up_relay=up_relay,
        s1=s1,
        gate_last=gate_last,
        up_other=up_other,
        s2=s2,
        tok_h=tok_h,
        up_other_relay=up_other_relay,
        s3=s3,
        gather_core=gather_core,
        tok_y=tok_y,
        s5=s5,
        core_arrive=core_arrive,
        hidden=hidden,
        s6=s6,
        grad_down=grad_down,
        s7=s7,
        wg=wg_grads,
        final=final,
    )
    for name, *at in SCHEDULE:
        steps[name](*at)
    for c in copies:
        c.wait_send()


def store(a, b, c, d, a_out, b_out, c_out, d_out, sem):
    moves = [
        pltpu.make_async_copy(src, dst, sem.at[i])
        for i, (src, dst) in enumerate(((b, b_out), (c, c_out), (d, d_out), (a, a_out)))
    ]
    for m in moves:
        m.start()
    for m in moves:
        m.wait()


def on_device(tokens, gate_pre, up_pre, grad_out, gate_weight, up_weight, down_weight):
    hbm = pl.BlockSpec(memory_space=pl.ANY)
    vmem = pl.BlockSpec(memory_space=pltpu.VMEM)
    bf = lambda *s: pltpu.VMEM(s, BF16)
    fl = lambda *s: pltpu.VMEM(s, F32)
    n = len(ORDER)
    made = pl.pallas_call(
        kernel,
        out_shape=(bf(64, FEAT), bf(FEAT, HID), bf(FEAT, HID), bf(HID, FEAT)),
        in_specs=[hbm] * 7,
        out_specs=(vmem,) * 4,
        scratch_shapes=[
            bf(FEAT, HID), bf(FEAT, HID), bf(HID, FEAT),
            bf(HID, FEAT), bf(HID, FEAT), bf(FEAT, HID),
            bf(4, 4, 64, FEAT), bf(4, 4, 64, FEAT),
            bf(8, 2, 64, HID), bf(8, 2, 64, HID),
            bf(4, PLANE, HID), bf(4, PLANE, HID), bf(4, PLANE, HID),
            bf(2, 4, PLANE, HALF),
            fl(n, CHUNK, HALF), fl(n, CHUNK, HALF), fl(n, CHUNK, HALF),
            bf(n, CHUNK, HALF), bf(n, 3, PART, HALF),
            fl(n, PART, HALF), bf(n, PART, HALF), bf(n, PART, HALF),
            bf(3, PLANE, FEAT), bf(3, PLANE, FEAT), fl(PLANE, FEAT),
            bf(PLANE, FEAT), bf(3, 64, FEAT),
            pltpu.SemaphoreType.DMA((N_COPY,)),
            pltpu.SemaphoreType.DMA((N_COPY,)),
            pltpu.SemaphoreType.DMA((8,)),
        ],
        compiler_params=pltpu.CompilerParams(
            collective_id=0, has_side_effects=True, vmem_limit_bytes=57 * 2**20
        ),
        cost_estimate=pl.CostEstimate(
            flops=12 * TOK * FEAT * HID, bytes_accessed=2**24, transcendentals=TOK * HID
        ),
        name="swiglu_backward",
    )(tokens, gate_pre, up_pre, grad_out, gate_weight, up_weight, down_weight)
    return pl.pallas_call(
        store,
        out_shape=tuple(jax.ShapeDtypeStruct(m.shape, BF16) for m in made),
        in_specs=[vmem] * 4,
        out_specs=(hbm,) * 4,
        scratch_shapes=[pltpu.SemaphoreType.DMA((4,))],
        compiler_params=pltpu.CompilerParams(vmem_limit_bytes=2**20),
        name="store",
    )(*(pltpu.with_memory_space_constraint(m, pltpu.VMEM) for m in made))


def solution(mesh):
    in_specs = (
        P("col", "row"),
        P("row", "col"),
        P("row", "col"),
        P("col", "row"),
        P("row", "col"),
        P("row", "col"),
        P("col", "row"),
    )
    out_specs = (P("col", "row"), P("row", "col"), P("row", "col"), P("col", "row"))
    return jax.shard_map(
        on_device, mesh=mesh, in_specs=in_specs, out_specs=out_specs, check_vma=False
    )
```

```python
import jax
import jax.numpy as jnp
from jax import lax
from jax.experimental import pallas as pl
from jax.experimental.pallas import tpu as pltpu
from jax.sharding import PartitionSpec as P

MESH = pl.DeviceIdType.MESH
F32 = jnp.float32
BF16 = jnp.bfloat16

NN = (((1,), (0,)), ((), ()))
TN = (((0,), (0,)), ((), ()))

TOK = 1024
FEAT = 512
HID = 1792
HALF = HID // 2
PLANE = 256
CHUNK = 128
PART = 32
ORDER = ((1, 0), (0, 0), (2, 1), (3, 0), (3, 1), (1, 1), (0, 1), (2, 0))
DIRECT = ((1, 0), (0, 0), (2, 1), (3, 0), (3, 1), (1, 1))
N_COPY = 192
SCHEDULE = (
    ("g_x",), ("uz",), ("u_x",), ("turn_down",), ("turn_up",), ("gz0",), ("g_relay",), ("gz12",),
    ("go_y",), ("s0", 1), ("s0", 6), ("u_other",), ("u_relay",), ("s0", 7), ("gz3",), ("s0", 0),
    ("s0", 4), ("s1", 7), ("s1", 0), ("s0", 3), ("u_other_relay",), ("s0", 5), ("s1", 3), ("s0", 2),
    ("s1", 5), ("s2", 7), ("s1", 4), ("s2", 0), ("gather_core",), ("tok_h",), ("s3", 7), ("s2", 3),
    ("s1", 2), ("s3", 0), ("s2", 5), ("s1", 1), ("s2", 4), ("s4", 7), ("s1", 6), ("s2", 2),
    ("tok_y",), ("s3", 3), ("s5", 0), ("s3", 5), ("core_arrive",), ("hidden",), ("s3", 2),
    ("s3", 4), ("grad_down",), ("s5", 7), ("s2", 1), ("s2", 6), ("s6", 0), ("s5", 3), ("s6", 7),
    ("s3", 1), ("s5", 5), ("s3", 6), ("s6", 3), ("s5", 2), ("s6", 5), ("s5", 4), ("s6", 2),
    ("s5", 1), ("s6", 4), ("s4", 6), ("s6", 1), ("s7", 0), ("s5", 6), ("s6", 6), ("s7", 1), ("wg",),
    ("final",),
)


def dot(a, b, dims):
    return lax.dot_general(a, b, dims, preferred_element_type=F32)


def ds(start, size):
    return pl.ds(pl.multiple_of(start, size), size)


def kernel(
    tok_in, gate_in, up_in, go_in, wg_in, wu_in, wd_in,
    gt_out, gg_out, gu_out, gd_out,
    wg, wu, wd, wg_t, wu_t, wd_t, tok, go, gate, up, hid, ggrad, ugrad, hg,
    keep, sib_send, sib_recv, x_send, x_recv, acc, z_send, z_recv,
    d_send, d_recv, d_sum, h_send, h_recv,
    send_sem, recv_sem, local_sem,
):
    row = lax.axis_index("row")
    col = lax.axis_index("col")
    zl, x, k = row // 8, (row // 2) % 4, row % 2
    y, zh = col // 4, col % 4
    chip = zl * 4 + x

    def dev(dzl=0, dx=0, dk=0, dy=0, dzh=0):
        return (
            ((zl + dzl) % 2) * 8 + ((x + dx) % 4) * 2 + (k + dk) % 2,
            ((y + dy) % 4) * 4 + (zh + dzh) % 4,
        )

    copies = []

    def prepare(src, dst, **offset):
        i = len(copies)
        cp = pltpu.make_async_remote_copy(
            src_ref=src, dst_ref=dst, send_sem=send_sem.at[i], recv_sem=recv_sem.at[i],
            device_id=dev(**offset), device_id_type=MESH,
        )
        copies.append(cp)
        return cp

    def send(src, dst, **offset):
        cp = prepare(src, dst, **offset)
        cp.start()
        return cp

    def arrive(group):
        for c in group:
            c.wait_recv()

    def both_ways(q):
        return send(q, q, dx=1), send(q, q, dx=3)

    def relay(pair, q_left, q_right, rows):
        pair[0].wait_recv()
        q = q_left(slice(0, rows // 2))
        to_right = send(q, q, dx=1)
        pair[1].wait_recv()
        q = q_right(slice(rows // 2, rows))
        return to_right, send(q, q, dx=3)

    locals_ = []

    def load(src, dst):
        cp = pltpu.make_async_copy(src, dst, local_sem.at[len(locals_)])
        cp.start()
        locals_.append(cp)
        return cp

    l_go = load(go_in, go.at[y, zh])

    peers = (
        [dict(dk=1), dict(dzl=1)]
        + [dict(dx=d) for d in (1, 2, 3)]
        + [dict(dy=d) for d in (1, 2, 3)]
        + [dict(dzh=d) for d in (1, 2, 3)]
    )
    barrier = pltpu.get_barrier_semaphore()
    for p in peers:
        pl.semaphore_signal(barrier, inc=1, device_id=dev(**p), device_id_type=MESH)
    pl.semaphore_wait(barrier, len(peers))

    other = (1 - zl) * 4 + x
    left, right, across = (zl * 4 + (x + d) % 4 for d in (3, 1, 2))
    o_left, o_right = ((1 - zl) * 4 + (x + d) % 4 for d in (3, 1))
    mine = ds(k * HALF, HALF)
    theirs = ds((1 - k) * HALF, HALF)
    st = [dict() for _ in ORDER]
    got = {}

    def plane(j):
        return (y + ORDER[j][0]) % 4

    def rows(j, start, size):
        return ds(ORDER[j][1] * CHUNK + start, size)

    def s0(j):
        dy, half = ORDER[j]
        if dy:
            got["go_y"][4 - dy, half].wait_recv()
        a = go[plane(j), 2 * half : 2 * half + 2].reshape(CHUNK, FEAT)
        sib_send[j] = dot(a, wd_t[:, theirs], NN)
        st[j]["sib"] = send(sib_send.at[j], sib_recv.at[j], dk=1)
        keep[j] = dot(a, wd_t[:, mine], NN)

    def s1(j):
        st[j]["sib"].wait_recv()

        @pl.loop(0, CHUNK // 16)
        def _(i):
            r = ds(i * 16, 16)
            x_send[j, r] = (keep[j, r] + sib_recv[j, r]).astype(BF16)

        st[j]["x"] = []
        for d in (2, 1, 3):
            r = ds((x + d) % 4 * PART, PART)
            st[j]["x"].append(send(x_send.at[j, r], x_recv.at[j, d - 1], dx=d))

    def s2(j):
        arrive(st[j]["x"])
        for i in range(PART // 16):
            r = pl.ds(i * 16, 16)
            o = ds(x * PART + i * 16, 16)
            t = keep[j, o] + sib_recv[j, o]
            for d in range(3):
                t = t + x_recv[j, d, r].astype(F32)
            acc[j, r] = t
            z_send[j, r] = t.astype(BF16)
        st[j]["z"] = send(z_send.at[j], z_recv.at[j], dzl=1)

    def s3(j):
        st[j]["z"].wait_recv()
        p = plane(j)
        for i in range(PART // 16):
            r = pl.ds(i * 16, 16)
            hg[k, p, rows(j, x * PART + i * 16, 16)] = (
                acc[j, r] + z_recv[j, r].astype(F32)
            ).astype(BF16)
        q = hg.at[k, p, rows(j, x * PART, PART)]
        if ORDER[j] in DIRECT:
            st[j]["ar"] = [send(q, q, dx=d) for d in (2, 1, 3)]
        else:
            st[j]["ag"] = both_ways(q)

    def s4(j):
        p = plane(j)

        def at(pos):
            return lambda r: hg.at[k, p, rows(j, pos % 4 * PART + r.start, 16)]

        st[j]["ar"] = relay(st[j]["ag"], at(x + 3), at(x + 1), PART)

    def s5(j):
        arrive(st[j]["ar"])
        q = hg.at[k, plane(j), rows(j, 0, CHUNK)]
        st[j]["core"] = send(q, q, dk=1)

    def s6(j):
        st[j]["core"].wait_recv()
        p = plane(j)
        dy, half = ORDER[j]
        for b in range(2):

            @pl.loop(0, 8, unroll=4)
            def _(i):
                r = ds(i // 2 * 16, 16)
                o = rows(j, b * 64 + i // 2 * 16, 16)
                h = i % 2
                c = ds(h * HALF, HALF)
                g = gate[2 * p + half, b, r, c].astype(F32)
                u = up[2 * p + half, b, r, c].astype(F32)
                t = hg[h, p, o].astype(F32)
                s = 1.0 / (1.0 + jnp.exp(-g))
                ts = t * s
                ggrad[p, o, c] = (ts * u * (1.0 + g * (1.0 - s))).astype(BF16)
                ugrad[p, o, c] = (ts * g).astype(BF16)

        o = rows(j, 0, CHUNK)
        part = dot(ggrad[p, o], wg_t[...], NN) + dot(ugrad[p, o], wu_t[...], NN)
        if dy:
            d_send[dy - 1, o] = part.astype(BF16)
            st[j]["d"] = send(d_send.at[dy - 1, o], d_recv.at[dy - 1, o], dy=dy)
        else:
            d_sum[o] = part

    def s7(half):
        for j, (dy, h) in enumerate(ORDER):
            if dy and h == half:
                st[j]["d"].wait_recv()
        o = pl.ds(half * CHUNK, CHUNK)
        t = d_sum[o]
        for d in range(3):
            t = t + d_recv[d, o].astype(F32)
        d_sum[o] = t
        h_send[o] = t.astype(BF16)
        for d, c in got["h"].items():

            @pl.when((zh + d) % 4 // 2 == half)
            def _():
                c.start()

    def hidden():
        @pl.loop(0, 64, unroll=4)
        def _(i):
            r = ds(i % 4 * 16, 16)
            b = i // 4
            o = ds(b % 4 * 64 + i % 4 * 16, 16)
            g = gate[b // 2, b % 2, r].astype(F32)
            u = up[b // 2, b % 2, r].astype(F32)
            hid[b // 4, o] = (g * u * (1.0 / (1.0 + jnp.exp(-g)))).astype(BF16)

    def grad_down():
        a, b = hid[...].reshape(TOK, HID), go[...].reshape(TOK, FEAT)
        gd_out[...] = dot(a, b, TN).astype(BF16)

    def tok_h():
        got["tok_h"] = [send(tok_in, tok.at[y, zh], dzh=d) for d in (2, 1, 3)]

    def tok_y():
        l_tok.wait()
        arrive(got["tok_h"])
        got["tok_y"] = [send(tok.at[y], tok.at[y], dy=d) for d in (2, 1, 3)]

    def g_x():
        q = gate.at[chip, k]
        got["g_x"] = send(gate_in, q, dx=1), send(gate_in, q, dx=3)

    def u_x():
        q = up.at[chip, k]
        got["u_x"] = send(up_in, q, dx=1), send(up_in, q, dx=3)

    def uz():
        got["u_z"] = send(up_in, up.at[chip, k], dzl=1)

    def gate_z(*places):
        got["g_z"] += [send(gate.at[at, k], gate.at[at, k], dzl=1) for at in places]

    def gz0():
        got["g_z"].append(send(gate_in, gate.at[chip, k], dzl=1))

    def g_relay():
        got["g_r"] = relay(
            got["g_x"], lambda r: gate.at[left, k, r], lambda r: gate.at[right, k, r], 64
        )

    def gz12():
        gate_z(left, right)

    def gz3():
        arrive(got["g_r"])
        gate_z(across)

    def u_relay():
        got["u_r"] = relay(
            got["u_x"], lambda r: up.at[left, k, r], lambda r: up.at[right, k, r], 64
        )

    def u_other():
        got["u_z"].wait_recv()
        got["u_x2"] = both_ways(up.at[other, k])

    def u_other_relay():
        got["u_r2"] = relay(
            got["u_x2"], lambda r: up.at[o_left, k, r], lambda r: up.at[o_right, k, r], 64
        )

    def gather_core():
        arrive(got["g_z"])
        arrive(got["u_r"])
        arrive(got["u_r2"])
        l_gate.wait()
        l_up.wait()
        got["core"] = [
            send(gate.at[:, k], gate.at[:, k], dk=1),
            send(up.at[:, k], up.at[:, k], dk=1),
        ]

    got["h"] = {
        d: prepare(h_send.at[ds((zh + d) % 4 * 64, 64)], h_recv.at[d - 1], dzh=d)
        for d in (2, 1, 3)
    }

    def go_y():
        arrive(go_h)
        l_go.wait()
        got["go_y"] = {}
        for d, h in ((2, 0), (3, 0), (1, 1), (1, 0), (3, 1), (2, 1)):
            q = go.at[y, 2 * h : 2 * h + 2]
            got["go_y"][d, h] = send(q, q, dy=d)

    def core_arrive():
        arrive(got["core"])

    def turn_down():
        l_wd.wait()
        wd_t[...] = wd[...].T

    def turn_up():
        l_wg.wait()
        l_wu.wait()
        wg_t[...] = wg[...].T
        wu_t[...] = wu[...].T

    def wg_grads():
        arrive(got["tok_y"])
        a = tok[...].reshape(TOK, FEAT)
        gg_out[...] = dot(a, ggrad[...].reshape(TOK, HID), TN).astype(BF16)
        gu_out[...] = dot(a, ugrad[...].reshape(TOK, HID), TN).astype(BF16)

    def final():
        arrive(got["h"].values())
        t = d_sum[ds(zh * 64, 64), :]
        for d in range(3):
            t = t + h_recv[d].astype(F32)
        gt_out[...] = t.astype(BF16)

    go_h = [send(go_in, go.at[y, zh], dzh=d) for d in (2, 1, 3)]
    got["g_z"] = []
    l_wd = load(wd_in, wd)
    l_gate = load(gate_in, gate.at[chip, k])
    l_up = load(up_in, up.at[chip, k])
    l_tok = load(tok_in, tok.at[y, zh])
    l_wg = load(wg_in, wg)
    l_wu = load(wu_in, wu)

    steps = dict(
        g_x=g_x,
        uz=uz,
        u_x=u_x,
        turn_down=turn_down,
        turn_up=turn_up,
        gz0=gz0,
        g_relay=g_relay,
        gz12=gz12,
        go_y=go_y,
        s0=s0,
        u_other=u_other,
        u_relay=u_relay,
        gz3=gz3,
        s1=s1,
        u_other_relay=u_other_relay,
        s2=s2,
        gather_core=gather_core,
        tok_h=tok_h,
        s3=s3,
        s4=s4,
        tok_y=tok_y,
        s5=s5,
        core_arrive=core_arrive,
        hidden=hidden,
        grad_down=grad_down,
        s6=s6,
        s7=s7,
        wg=wg_grads,
        final=final,
    )
    for name, *at in SCHEDULE:
        steps[name](*at)
    for c in copies:
        c.wait_send()


def store(a, b, c, d, a_out, b_out, c_out, d_out, sem):
    moves = [
        pltpu.make_async_copy(src, dst, sem.at[i])
        for i, (src, dst) in enumerate(((b, b_out), (c, c_out), (d, d_out), (a, a_out)))
    ]
    for m in moves:
        m.start()
    for m in moves:
        m.wait()


def on_device(tokens, gate_pre, up_pre, grad_out, gate_weight, up_weight, down_weight):
    hbm = pl.BlockSpec(memory_space=pl.ANY)
    vmem = pl.BlockSpec(memory_space=pltpu.VMEM)
    bf = lambda *s: pltpu.VMEM(s, BF16)
    fl = lambda *s: pltpu.VMEM(s, F32)
    n = len(ORDER)
    made = pl.pallas_call(
        kernel,
        out_shape=(bf(64, FEAT), bf(FEAT, HID), bf(FEAT, HID), bf(HID, FEAT)),
        in_specs=[hbm] * 7,
        out_specs=(vmem,) * 4,
        scratch_shapes=[
            bf(FEAT, HID), bf(FEAT, HID), bf(HID, FEAT),
            bf(HID, FEAT), bf(HID, FEAT), bf(FEAT, HID),
            bf(4, 4, 64, FEAT), bf(4, 4, 64, FEAT),
            bf(8, 2, 64, HID), bf(8, 2, 64, HID),
            bf(4, PLANE, HID), bf(4, PLANE, HID), bf(4, PLANE, HID),
            bf(2, 4, PLANE, HALF),
            fl(n, CHUNK, HALF), fl(n, CHUNK, HALF), fl(n, CHUNK, HALF),
            bf(n, CHUNK, HALF), bf(n, 3, PART, HALF),
            fl(n, PART, HALF), bf(n, PART, HALF), bf(n, PART, HALF),
            bf(3, PLANE, FEAT), bf(3, PLANE, FEAT), fl(PLANE, FEAT),
            bf(PLANE, FEAT), bf(3, 64, FEAT),
            pltpu.SemaphoreType.DMA((N_COPY,)),
            pltpu.SemaphoreType.DMA((N_COPY,)),
            pltpu.SemaphoreType.DMA((8,)),
        ],
        compiler_params=pltpu.CompilerParams(
            collective_id=0, has_side_effects=True, vmem_limit_bytes=57 * 2**20
        ),
        cost_estimate=pl.CostEstimate(
            flops=12 * TOK * FEAT * HID, bytes_accessed=2**24, transcendentals=TOK * HID
        ),
        name="swiglu_backward",
    )(tokens, gate_pre, up_pre, grad_out, gate_weight, up_weight, down_weight)
    return pl.pallas_call(
        store,
        out_shape=tuple(jax.ShapeDtypeStruct(m.shape, BF16) for m in made),
        in_specs=[vmem] * 4,
        out_specs=(hbm,) * 4,
        scratch_shapes=[pltpu.SemaphoreType.DMA((4,))],
        compiler_params=pltpu.CompilerParams(vmem_limit_bytes=2**20),
        name="store",
    )(*(pltpu.with_memory_space_constraint(m, pltpu.VMEM) for m in made))


def solution(mesh):
    in_specs = (
        P("col", "row"),
        P("row", "col"),
        P("row", "col"),
        P("col", "row"),
        P("row", "col"),
        P("row", "col"),
        P("col", "row"),
    )
    out_specs = (P("col", "row"), P("row", "col"), P("row", "col"), P("col", "row"))
    return jax.shard_map(
        on_device, mesh=mesh, in_specs=in_specs, out_specs=out_specs, check_vma=False
    )
```

```python
import jax
import jax.numpy as jnp
from jax import lax
from jax.experimental import pallas as pl
from jax.experimental.pallas import tpu as pltpu
from jax.sharding import PartitionSpec as P

MESH = pl.DeviceIdType.MESH
F32 = jnp.float32
BF16 = jnp.bfloat16

NN = (((1,), (0,)), ((), ()))
TN = (((0,), (0,)), ((), ()))

TOK = 1024
FEAT = 512
HID = 1792
HALF = HID // 2
PLANE = 256
CHUNK = 128
PART = 32
ORDER = ((3, 0), (0, 0), (2, 1), (1, 1), (2, 0), (0, 1), (1, 0), (3, 1))
DIRECT = ((0, 0), (1, 1), (0, 1), (1, 0), (3, 1))
N_COPY = 192
SCHEDULE = (
    ("u_x",), ("uz",), ("g_x",), ("turn_down",), ("turn_up",), ("u_relay",), ("tok_h",), ("go_y",),
    ("s0", 1), ("s0", 5), ("g_relay",), ("gz12",), ("u_other",), ("s0", 2), ("s0", 3), ("gz3",),
    ("s1", 2), ("s0", 0), ("s0", 4), ("s1", 0), ("s0", 6), ("s0", 7), ("s1", 4), ("s2", 2),
    ("s1", 6), ("s2", 0), ("u_other_relay",), ("s1", 7), ("s2", 4), ("gz0",), ("s2", 6), ("s3", 2),
    ("s3", 0), ("tok_y",), ("s3", 4), ("s2", 7), ("s1", 3), ("s4", 2), ("s1", 1), ("s4", 0),
    ("s4", 4), ("gather_core",), ("s3", 6), ("s2", 3), ("s1", 5), ("s5", 2), ("s3", 7), ("s2", 1),
    ("s5", 0), ("s3", 3), ("s5", 4), ("core_arrive",), ("s6", 2), ("s5", 6), ("s3", 1), ("s6", 0),
    ("s2", 5), ("s6", 4), ("s5", 7), ("s6", 6), ("s5", 3), ("s3", 5), ("s6", 7), ("s5", 1),
    ("s6", 3), ("s6", 1), ("s7", 0), ("s5", 5), ("s6", 5), ("s7", 1), ("wg",), ("final",),
)


def dot(a, b, dims):
    return lax.dot_general(a, b, dims, preferred_element_type=F32)


def ds(start, size):
    return pl.ds(pl.multiple_of(start, size), size)


def kernel(
    tok_in, gate_in, up_in, go_in, wg_in, wu_in, wd_in,
    gt_out, gg_out, gu_out, hid, go_out,
    wg, wu, wd, wg_t, wu_t, wd_t, tok, go, gate, up, ggrad, ugrad, hg,
    keep, sib_send, sib_recv, x_send, x_recv, acc, z_send, z_recv,
    d_send, d_recv, d_sum, h_send, h_recv,
    send_sem, recv_sem, local_sem,
):
    row = lax.axis_index("row")
    col = lax.axis_index("col")
    zl, x, k = row // 8, (row // 2) % 4, row % 2
    y, zh = col // 4, col % 4
    chip = zl * 4 + x

    def dev(dzl=0, dx=0, dk=0, dy=0, dzh=0):
        return (
            ((zl + dzl) % 2) * 8 + ((x + dx) % 4) * 2 + (k + dk) % 2,
            ((y + dy) % 4) * 4 + (zh + dzh) % 4,
        )

    copies = []

    def prepare(src, dst, **offset):
        i = len(copies)
        cp = pltpu.make_async_remote_copy(
            src_ref=src, dst_ref=dst, send_sem=send_sem.at[i], recv_sem=recv_sem.at[i],
            device_id=dev(**offset), device_id_type=MESH,
        )
        copies.append(cp)
        return cp

    def send(src, dst, **offset):
        cp = prepare(src, dst, **offset)
        cp.start()
        return cp

    def arrive(group):
        for c in group:
            c.wait_recv()

    def both_ways(q):
        return send(q, q, dx=1), send(q, q, dx=3)

    def relay(pair, q_left, q_right, rows):
        pair[0].wait_recv()
        q = q_left(slice(0, rows // 2))
        to_right = send(q, q, dx=1)
        pair[1].wait_recv()
        q = q_right(slice(rows // 2, rows))
        return to_right, send(q, q, dx=3)

    locals_ = []

    def load(src, dst):
        cp = pltpu.make_async_copy(src, dst, local_sem.at[len(locals_)])
        cp.start()
        locals_.append(cp)
        return cp

    l_go = load(go_in, go.at[y, zh])

    peers = (
        [dict(dk=1), dict(dzl=1)]
        + [dict(dx=d) for d in (1, 2, 3)]
        + [dict(dy=d) for d in (1, 2, 3)]
        + [dict(dzh=d) for d in (1, 2, 3)]
    )
    barrier = pltpu.get_barrier_semaphore()
    for p in peers:
        pl.semaphore_signal(barrier, inc=1, device_id=dev(**p), device_id_type=MESH)
    pl.semaphore_wait(barrier, len(peers))

    other = (1 - zl) * 4 + x
    left, right, across = (zl * 4 + (x + d) % 4 for d in (3, 1, 2))
    o_left, o_right = ((1 - zl) * 4 + (x + d) % 4 for d in (3, 1))
    mine = ds(k * HALF, HALF)
    theirs = ds((1 - k) * HALF, HALF)
    st = [dict() for _ in ORDER]
    got = {}

    def plane(j):
        return (y + ORDER[j][0]) % 4

    def rows(j, start, size):
        return ds(ORDER[j][1] * CHUNK + start, size)

    def s0(j):
        dy, half = ORDER[j]
        if dy:
            got["go_y"][4 - dy, half].wait_recv()
        a = go[plane(j), 2 * half : 2 * half + 2].reshape(CHUNK, FEAT)
        sib_send[j] = dot(a, wd_t[:, theirs], NN)
        st[j]["sib"] = send(sib_send.at[j], sib_recv.at[j], dk=1)
        keep[j] = dot(a, wd_t[:, mine], NN)

    def s1(j):
        st[j]["sib"].wait_recv()

        @pl.loop(0, CHUNK // 16)
        def _(i):
            r = ds(i * 16, 16)
            x_send[j, r] = (keep[j, r] + sib_recv[j, r]).astype(BF16)

        st[j]["x"] = []
        for d in (2, 1, 3):
            r = ds((x + d) % 4 * PART, PART)
            st[j]["x"].append(send(x_send.at[j, r], x_recv.at[j, d - 1], dx=d))

    def s2(j):
        arrive(st[j]["x"])
        for i in range(PART // 16):
            r = pl.ds(i * 16, 16)
            o = ds(x * PART + i * 16, 16)
            t = keep[j, o] + sib_recv[j, o]
            for d in range(3):
                t = t + x_recv[j, d, r].astype(F32)
            acc[j, r] = t
            z_send[j, r] = t.astype(BF16)
        st[j]["z"] = send(z_send.at[j], z_recv.at[j], dzl=1)

    def s3(j):
        st[j]["z"].wait_recv()
        p = plane(j)
        for i in range(PART // 16):
            r = pl.ds(i * 16, 16)
            hg[k, p, rows(j, x * PART + i * 16, 16)] = (
                acc[j, r] + z_recv[j, r].astype(F32)
            ).astype(BF16)
        q = hg.at[k, p, rows(j, x * PART, PART)]
        if ORDER[j] in DIRECT:
            st[j]["ar"] = [send(q, q, dx=d) for d in (2, 1, 3)]
        else:
            st[j]["ag"] = both_ways(q)

    def s4(j):
        p = plane(j)

        def at(pos):
            return lambda r: hg.at[k, p, rows(j, pos % 4 * PART + r.start, 16)]

        st[j]["ar"] = relay(st[j]["ag"], at(x + 3), at(x + 1), PART)

    def s5(j):
        arrive(st[j]["ar"])
        q = hg.at[k, plane(j), rows(j, 0, CHUNK)]
        st[j]["core"] = send(q, q, dk=1)

    def s6(j):
        st[j]["core"].wait_recv()
        p = plane(j)
        dy, half = ORDER[j]
        for b in range(2):

            @pl.loop(0, 8, unroll=4)
            def _(i):
                r = ds(i // 2 * 16, 16)
                o = rows(j, b * 64 + i // 2 * 16, 16)
                h = i % 2
                c = ds(h * HALF, HALF)
                g = gate[2 * p + half, b, r, c].astype(F32)
                u = up[2 * p + half, b, r, c].astype(F32)
                t = hg[h, p, o].astype(F32)
                s = 1.0 / (1.0 + jnp.exp(-g))
                ts = t * s
                ggrad[p, o, c] = (ts * u * (1.0 + g * (1.0 - s))).astype(BF16)
                ugrad[p, o, c] = (ts * g).astype(BF16)
                hid[p, o, c] = (g * s * u).astype(BF16)

        o = rows(j, 0, CHUNK)
        part = dot(ggrad[p, o], wg_t[...], NN) + dot(ugrad[p, o], wu_t[...], NN)
        if dy:
            d_send[dy - 1, o] = part.astype(BF16)
            st[j]["d"] = send(d_send.at[dy - 1, o], d_recv.at[dy - 1, o], dy=dy)
        else:
            d_sum[o] = part

    def s7(half):
        for j, (dy, h) in enumerate(ORDER):
            if dy and h == half:
                st[j]["d"].wait_recv()
        o = pl.ds(half * CHUNK, CHUNK)
        t = d_sum[o]
        for d in range(3):
            t = t + d_recv[d, o].astype(F32)
        d_sum[o] = t
        h_send[o] = t.astype(BF16)
        for d, c in got["h"].items():

            @pl.when((zh + d) % 4 // 2 == half)
            def _():
                c.start()

    def tok_h():
        got["tok_h"] = [send(tok_in, tok.at[y, zh], dzh=d) for d in (2, 1, 3)]

    def tok_y():
        l_tok.wait()
        arrive(got["tok_h"])
        got["tok_y"] = [send(tok.at[y], tok.at[y], dy=d) for d in (2, 1, 3)]

    def g_x():
        q = gate.at[chip, k]
        got["g_x"] = send(gate_in, q, dx=1), send(gate_in, q, dx=3)

    def u_x():
        q = up.at[chip, k]
        got["u_x"] = send(up_in, q, dx=1), send(up_in, q, dx=3)

    def uz():
        got["u_z"] = send(up_in, up.at[chip, k], dzl=1)

    def gate_z(*places):
        got["g_z"] += [send(gate.at[at, k], gate.at[at, k], dzl=1) for at in places]

    def gz0():
        got["g_z"].append(send(gate_in, gate.at[chip, k], dzl=1))

    def g_relay():
        got["g_r"] = relay(
            got["g_x"], lambda r: gate.at[left, k, r], lambda r: gate.at[right, k, r], 64
        )

    def gz12():
        gate_z(left, right)

    def gz3():
        arrive(got["g_r"])
        gate_z(across)

    def u_relay():
        got["u_r"] = relay(
            got["u_x"], lambda r: up.at[left, k, r], lambda r: up.at[right, k, r], 64
        )

    def u_other():
        got["u_z"].wait_recv()
        got["u_x2"] = both_ways(up.at[other, k])

    def u_other_relay():
        got["u_r2"] = relay(
            got["u_x2"], lambda r: up.at[o_left, k, r], lambda r: up.at[o_right, k, r], 64
        )

    def gather_core():
        arrive(got["g_z"])
        arrive(got["u_r"])
        arrive(got["u_r2"])
        l_gate.wait()
        l_up.wait()
        got["core"] = [
            send(gate.at[:, k], gate.at[:, k], dk=1),
            send(up.at[:, k], up.at[:, k], dk=1),
        ]

    got["h"] = {
        d: prepare(h_send.at[ds((zh + d) % 4 * 64, 64)], h_recv.at[d - 1], dzh=d)
        for d in (2, 1, 3)
    }

    def go_y():
        arrive(go_h)
        l_go.wait()
        got["go_y"] = {}
        for d, h in ((2, 1), (3, 1), (2, 0), (1, 0), (1, 1), (3, 0)):
            q = go.at[y, 2 * h : 2 * h + 2]
            got["go_y"][d, h] = send(q, q, dy=d)

    def core_arrive():
        arrive(got["core"])
        go_out[...] = go[...]

    def turn_down():
        l_wd.wait()
        wd_t[...] = wd[...].T

    def turn_up():
        l_wg.wait()
        l_wu.wait()
        wg_t[...] = wg[...].T
        wu_t[...] = wu[...].T

    def wg_grads():
        arrive(got["tok_y"])
        a = tok[...].reshape(TOK, FEAT)
        gg_out[...] = dot(a, ggrad[...].reshape(TOK, HID), TN).astype(BF16)
        gu_out[...] = dot(a, ugrad[...].reshape(TOK, HID), TN).astype(BF16)

    def final():
        arrive(got["h"].values())
        t = d_sum[ds(zh * 64, 64), :]
        for d in range(3):
            t = t + h_recv[d].astype(F32)
        gt_out[...] = t.astype(BF16)

    go_h = [send(go_in, go.at[y, zh], dzh=d) for d in (2, 1, 3)]
    got["g_z"] = []
    l_wd = load(wd_in, wd)
    l_gate = load(gate_in, gate.at[chip, k])
    l_up = load(up_in, up.at[chip, k])
    l_tok = load(tok_in, tok.at[y, zh])
    l_wg = load(wg_in, wg)
    l_wu = load(wu_in, wu)

    steps = dict(
        u_x=u_x,
        uz=uz,
        g_x=g_x,
        turn_down=turn_down,
        turn_up=turn_up,
        u_relay=u_relay,
        tok_h=tok_h,
        go_y=go_y,
        s0=s0,
        g_relay=g_relay,
        gz12=gz12,
        u_other=u_other,
        gz3=gz3,
        s1=s1,
        s2=s2,
        u_other_relay=u_other_relay,
        gz0=gz0,
        s3=s3,
        tok_y=tok_y,
        s4=s4,
        gather_core=gather_core,
        s5=s5,
        core_arrive=core_arrive,
        s6=s6,
        s7=s7,
        wg=wg_grads,
        final=final,
    )
    for name, *at in SCHEDULE:
        steps[name](*at)
    for c in copies:
        c.wait_send()


def finish(gt, gg, gu, hid, go, gt_out, gg_out, gu_out, gd_out, gd, sem):
    moves = []

    def move(src, dst):
        moves.append(pltpu.make_async_copy(src, dst, sem.at[len(moves)]))
        moves[-1].start()

    for src, dst in ((gg, gg_out), (gu, gu_out)):
        for i in range(2):
            r = pl.ds(i * FEAT // 2, FEAT // 2)
            move(src.at[r], dst.at[r])
    move(gt, gt_out)
    b = go[...].reshape(TOK, FEAT)
    for i in range(7):
        r = pl.ds(i * 256, 256)
        gd[r] = dot(hid[:, :, r].reshape(TOK, 256), b, TN).astype(BF16)
        move(gd.at[r], gd_out.at[r])
    for m in moves:
        m.wait()


def on_device(tokens, gate_pre, up_pre, grad_out, gate_weight, up_weight, down_weight):
    hbm = pl.BlockSpec(memory_space=pl.ANY)
    vmem = pl.BlockSpec(memory_space=pltpu.VMEM)
    bf = lambda *s: pltpu.VMEM(s, BF16)
    fl = lambda *s: pltpu.VMEM(s, F32)
    n = len(ORDER)
    made = pl.pallas_call(
        kernel,
        out_shape=(
            bf(64, FEAT), bf(FEAT, HID), bf(FEAT, HID), bf(4, PLANE, HID), bf(4, 4, 64, FEAT)
        ),
        in_specs=[hbm] * 7,
        out_specs=(vmem,) * 5,
        scratch_shapes=[
            bf(FEAT, HID), bf(FEAT, HID), bf(HID, FEAT),
            bf(HID, FEAT), bf(HID, FEAT), bf(FEAT, HID),
            bf(4, 4, 64, FEAT), bf(4, 4, 64, FEAT),
            bf(8, 2, 64, HID), bf(8, 2, 64, HID),
            bf(4, PLANE, HID), bf(4, PLANE, HID),
            bf(2, 4, PLANE, HALF),
            fl(n, CHUNK, HALF), fl(n, CHUNK, HALF), fl(n, CHUNK, HALF),
            bf(n, CHUNK, HALF), bf(n, 3, PART, HALF),
            fl(n, PART, HALF), bf(n, PART, HALF), bf(n, PART, HALF),
            bf(3, PLANE, FEAT), bf(3, PLANE, FEAT), fl(PLANE, FEAT),
            bf(PLANE, FEAT), bf(3, 64, FEAT),
            pltpu.SemaphoreType.DMA((N_COPY,)),
            pltpu.SemaphoreType.DMA((N_COPY,)),
            pltpu.SemaphoreType.DMA((8,)),
        ],
        compiler_params=pltpu.CompilerParams(
            collective_id=0, has_side_effects=True, vmem_limit_bytes=53 * 2**20
        ),
        cost_estimate=pl.CostEstimate(
            flops=10 * TOK * FEAT * HID, bytes_accessed=2**24, transcendentals=TOK * HID
        ),
        name="swiglu_backward",
    )(tokens, gate_pre, up_pre, grad_out, gate_weight, up_weight, down_weight)
    return pl.pallas_call(
        finish,
        out_shape=tuple(
            jax.ShapeDtypeStruct(shape, BF16)
            for shape in ((64, FEAT), (FEAT, HID), (FEAT, HID), (HID, FEAT))
        ),
        in_specs=[vmem] * 5,
        out_specs=(hbm,) * 4,
        scratch_shapes=[bf(HID, FEAT), pltpu.SemaphoreType.DMA((12,))],
        compiler_params=pltpu.CompilerParams(vmem_limit_bytes=10 * 2**20),
        name="finish",
    )(*(pltpu.with_memory_space_constraint(m, pltpu.VMEM) for m in made))


def solution(mesh):
    in_specs = (
        P("col", "row"),
        P("row", "col"),
        P("row", "col"),
        P("col", "row"),
        P("row", "col"),
        P("row", "col"),
        P("col", "row"),
    )
    out_specs = (P("col", "row"), P("row", "col"), P("row", "col"), P("col", "row"))
    return jax.shard_map(
        on_device, mesh=mesh, in_specs=in_specs, out_specs=out_specs, check_vma=False
    )
```

```python
import jax
import jax.numpy as jnp
from jax import lax
from jax.experimental import pallas as pl
from jax.experimental.pallas import tpu as pltpu
from jax.sharding import PartitionSpec as P

MESH = pl.DeviceIdType.MESH
F32 = jnp.float32
BF16 = jnp.bfloat16

NN = (((1,), (0,)), ((), ()))
TN = (((0,), (0,)), ((), ()))

TOK = 1024
FEAT = 512
HID = 1792
HALF = HID // 2
PLANE = 256
CHUNK = 128
PART = 32
ORDER = ((3, 0), (0, 0), (2, 1), (1, 1), (2, 0), (0, 1), (1, 0), (3, 1))
DIRECT = ((0, 0), (1, 1), (0, 1), (1, 0), (3, 1))
N_COPY = 192
SCHEDULE = (
    ("u_x",), ("uz",), ("g_x",), ("turn_down",), ("turn_up",), ("u_relay",), ("tok_h",), ("go_y",),
    ("s0", 1), ("s0", 5), ("g_relay",), ("gz12",), ("u_other",), ("s0", 2), ("s0", 3), ("gz3",),
    ("s1", 2), ("s0", 0), ("s0", 4), ("s1", 0), ("s0", 6), ("s0", 7), ("s1", 4), ("s2", 2),
    ("s1", 6), ("s2", 0), ("u_other_relay",), ("s1", 7), ("s2", 4), ("gz0",), ("s2", 6), ("s3", 2),
    ("s3", 0), ("tok_y",), ("s3", 4), ("s2", 7), ("s1", 3), ("s4", 2), ("s1", 1), ("s4", 0),
    ("s4", 4), ("gather_core",), ("s3", 6), ("s2", 3), ("s1", 5), ("s5", 2), ("s3", 7), ("s2", 1),
    ("s5", 0), ("s3", 3), ("s5", 4), ("core_arrive",), ("s6", 2), ("s5", 6), ("s3", 1), ("s6", 0),
    ("s2", 5), ("s6", 4), ("s5", 7), ("s6", 6), ("s5", 3), ("s3", 5), ("s6", 7), ("s5", 1),
    ("s6", 3), ("s6", 1), ("s7", 0), ("s5", 5), ("s6", 5), ("s7", 1), ("wg",), ("final",),
)


def dot(a, b, dims):
    return lax.dot_general(a, b, dims, preferred_element_type=F32)


def ds(start, size):
    return pl.ds(pl.multiple_of(start, size), size)


def kernel(
    tok_in, gate_in, up_in, go_in, wg_in, wu_in, wd_in,
    gt_out, gg_out, gu_out, hid, go_out,
    wg, wu, wd, wg_t, wu_t, wd_t, tok, go, gate, up, ggrad, ugrad, hg,
    keep, sib_send, sib_recv, x_send, x_recv, acc, z_send, z_recv,
    d_send, d_recv, d_sum, h_send, h_recv,
    send_sem, recv_sem, local_sem,
):
    row = lax.axis_index("row")
    col = lax.axis_index("col")
    zl, x, k = row // 8, (row // 2) % 4, row % 2
    y, zh = col // 4, col % 4
    chip = zl * 4 + x

    def dev(dzl=0, dx=0, dk=0, dy=0, dzh=0):
        return (
            ((zl + dzl) % 2) * 8 + ((x + dx) % 4) * 2 + (k + dk) % 2,
            ((y + dy) % 4) * 4 + (zh + dzh) % 4,
        )

    copies = []

    def prepare(src, dst, **offset):
        i = len(copies)
        cp = pltpu.make_async_remote_copy(
            src_ref=src, dst_ref=dst, send_sem=send_sem.at[i], recv_sem=recv_sem.at[i],
            device_id=dev(**offset), device_id_type=MESH,
        )
        copies.append(cp)
        return cp

    def send(src, dst, **offset):
        cp = prepare(src, dst, **offset)
        cp.start()
        return cp

    def arrive(group):
        for c in group:
            c.wait_recv()

    def both_ways(q):
        return send(q, q, dx=1), send(q, q, dx=3)

    def relay(pair, q_left, q_right, rows):
        pair[0].wait_recv()
        q = q_left(slice(0, rows // 2))
        to_right = send(q, q, dx=1)
        pair[1].wait_recv()
        q = q_right(slice(rows // 2, rows))
        return to_right, send(q, q, dx=3)

    locals_ = []

    def load(src, dst):
        cp = pltpu.make_async_copy(src, dst, local_sem.at[len(locals_)])
        cp.start()
        locals_.append(cp)
        return cp

    l_go = load(go_in, go.at[y, zh])

    peers = (
        [dict(dk=1), dict(dzl=1)]
        + [dict(dx=d) for d in (1, 2, 3)]
        + [dict(dy=d) for d in (1, 2, 3)]
        + [dict(dzh=d) for d in (1, 2, 3)]
    )
    barrier = pltpu.get_barrier_semaphore()
    for p in peers:
        pl.semaphore_signal(barrier, inc=1, device_id=dev(**p), device_id_type=MESH)
    pl.semaphore_wait(barrier, len(peers))

    other = (1 - zl) * 4 + x
    left, right, across = (zl * 4 + (x + d) % 4 for d in (3, 1, 2))
    o_left, o_right = ((1 - zl) * 4 + (x + d) % 4 for d in (3, 1))
    mine = ds(k * HALF, HALF)
    theirs = ds((1 - k) * HALF, HALF)
    st = [dict() for _ in ORDER]
    got = {}

    def plane(j):
        return (y + ORDER[j][0]) % 4

    def rows(j, start, size):
        return ds(ORDER[j][1] * CHUNK + start, size)

    def s0(j):
        dy, half = ORDER[j]
        if dy:
            got["go_y"][4 - dy, half].wait_recv()
        a = go[plane(j), 2 * half : 2 * half + 2].reshape(CHUNK, FEAT)
        sib_send[j] = dot(a, wd_t[:, theirs], NN)
        st[j]["sib"] = send(sib_send.at[j], sib_recv.at[j], dk=1)
        keep[j] = dot(a, wd_t[:, mine], NN)

    def s1(j):
        st[j]["sib"].wait_recv()

        @pl.loop(0, CHUNK // 16, unroll=True)
        def _(i):
            r = ds(i * 16, 16)
            x_send[j, r] = (keep[j, r] + sib_recv[j, r]).astype(BF16)

        st[j]["x"] = []
        for d in (2, 1, 3):
            r = ds((x + d) % 4 * PART, PART)
            st[j]["x"].append(send(x_send.at[j, r], x_recv.at[j, d - 1], dx=d))

    def s2(j):
        arrive(st[j]["x"])
        for i in range(PART // 16):
            r = pl.ds(i * 16, 16)
            o = ds(x * PART + i * 16, 16)
            t = keep[j, o] + sib_recv[j, o]
            for d in range(3):
                t = t + x_recv[j, d, r].astype(F32)
            acc[j, r] = t
            z_send[j, r] = t.astype(BF16)
        st[j]["z"] = send(z_send.at[j], z_recv.at[j], dzl=1)

    def s3(j):
        st[j]["z"].wait_recv()
        p = plane(j)
        for i in range(PART // 16):
            r = pl.ds(i * 16, 16)
            hg[k, p, rows(j, x * PART + i * 16, 16)] = (
                acc[j, r] + z_recv[j, r].astype(F32)
            ).astype(BF16)
        q = hg.at[k, p, rows(j, x * PART, PART)]
        if ORDER[j] in DIRECT:
            st[j]["ar"] = [send(q, q, dx=d) for d in (2, 1, 3)]
        else:
            st[j]["ag"] = both_ways(q)

    def s4(j):
        p = plane(j)

        def at(pos):
            return lambda r: hg.at[k, p, rows(j, pos % 4 * PART + r.start, 16)]

        st[j]["ar"] = relay(st[j]["ag"], at(x + 3), at(x + 1), PART)

    def s5(j):
        arrive(st[j]["ar"])
        q = hg.at[k, plane(j), rows(j, 0, CHUNK)]
        st[j]["core"] = send(q, q, dk=1)

    def s6(j):
        st[j]["core"].wait_recv()
        p = plane(j)
        dy, half = ORDER[j]
        for b in range(2):

            @pl.loop(0, 8, unroll=True)
            def _(i):
                r = ds(i // 2 * 16, 16)
                o = rows(j, b * 64 + i // 2 * 16, 16)
                h = i % 2
                c = ds(h * HALF, HALF)
                g = gate[2 * p + half, b, r, c].astype(F32)
                u = up[2 * p + half, b, r, c].astype(F32)
                t = hg[h, p, o].astype(F32)
                s = 1.0 / (1.0 + jnp.exp(-g))
                ts = t * s
                ggrad[p, o, c] = (ts * u * (1.0 + g * (1.0 - s))).astype(BF16)
                ugrad[p, o, c] = (ts * g).astype(BF16)
                hid[p, o, c] = (g * s * u).astype(BF16)

        o = rows(j, 0, CHUNK)
        part = dot(ggrad[p, o], wg_t[...], NN) + dot(ugrad[p, o], wu_t[...], NN)
        if dy:
            d_send[dy - 1, o] = part.astype(BF16)
            st[j]["d"] = send(d_send.at[dy - 1, o], d_recv.at[dy - 1, o], dy=dy)
        else:
            d_sum[o] = part

    def s7(half):
        for j, (dy, h) in enumerate(ORDER):
            if dy and h == half:
                st[j]["d"].wait_recv()
        o = pl.ds(half * CHUNK, CHUNK)
        t = d_sum[o]
        for d in range(3):
            t = t + d_recv[d, o].astype(F32)
        d_sum[o] = t
        h_send[o] = t.astype(BF16)
        for d, c in got["h"].items():

            @pl.when((zh + d) % 4 // 2 == half)
            def _():
                c.start()

    def tok_h():
        got["tok_h"] = [send(tok_in, tok.at[y, zh], dzh=d) for d in (2, 1, 3)]

    def tok_y():
        l_tok.wait()
        arrive(got["tok_h"])
        got["tok_y"] = [send(tok.at[y], tok.at[y], dy=d) for d in (2, 1, 3)]

    def g_x():
        q = gate.at[chip, k]
        got["g_x"] = send(gate_in, q, dx=1), send(gate_in, q, dx=3)

    def u_x():
        q = up.at[chip, k]
        got["u_x"] = send(up_in, q, dx=1), send(up_in, q, dx=3)

    def uz():
        got["u_z"] = send(up_in, up.at[chip, k], dzl=1)

    def gate_z(*places):
        got["g_z"] += [send(gate.at[at, k], gate.at[at, k], dzl=1) for at in places]

    def gz0():
        got["g_z"].append(send(gate_in, gate.at[chip, k], dzl=1))

    def g_relay():
        got["g_r"] = relay(
            got["g_x"], lambda r: gate.at[left, k, r], lambda r: gate.at[right, k, r], 64
        )

    def gz12():
        gate_z(left, right)

    def gz3():
        arrive(got["g_r"])
        gate_z(across)

    def u_relay():
        got["u_r"] = relay(
            got["u_x"], lambda r: up.at[left, k, r], lambda r: up.at[right, k, r], 64
        )

    def u_other():
        got["u_z"].wait_recv()
        got["u_x2"] = both_ways(up.at[other, k])

    def u_other_relay():
        got["u_r2"] = relay(
            got["u_x2"], lambda r: up.at[o_left, k, r], lambda r: up.at[o_right, k, r], 64
        )

    def gather_core():
        arrive(got["g_z"])
        arrive(got["u_r"])
        arrive(got["u_r2"])
        l_gate.wait()
        l_up.wait()
        got["core"] = [
            send(gate.at[:, k], gate.at[:, k], dk=1),
            send(up.at[:, k], up.at[:, k], dk=1),
        ]

    got["h"] = {
        d: prepare(h_send.at[ds((zh + d) % 4 * 64, 64)], h_recv.at[d - 1], dzh=d)
        for d in (2, 1, 3)
    }

    def go_y():
        arrive(go_h)
        l_go.wait()
        got["go_y"] = {}
        for d, h in ((2, 1), (3, 1), (2, 0), (1, 0), (1, 1), (3, 0)):
            q = go.at[y, 2 * h : 2 * h + 2]
            got["go_y"][d, h] = send(q, q, dy=d)

    def core_arrive():
        arrive(got["core"])
        go_out[...] = go[...]

    def turn_down():
        l_wd.wait()
        wd_t[...] = wd[...].T

    def turn_up():
        l_wg.wait()
        l_wu.wait()
        wg_t[...] = wg[...].T
        wu_t[...] = wu[...].T

    def wg_grads():
        arrive(got["tok_y"])
        a = tok[...].reshape(TOK, FEAT)
        gg_out[...] = dot(a, ggrad[...].reshape(TOK, HID), TN).astype(BF16)
        gu_out[...] = dot(a, ugrad[...].reshape(TOK, HID), TN).astype(BF16)

    def final():
        arrive(got["h"].values())
        t = d_sum[ds(zh * 64, 64), :]
        for d in range(3):
            t = t + h_recv[d].astype(F32)
        gt_out[...] = t.astype(BF16)

    go_h = [send(go_in, go.at[y, zh], dzh=d) for d in (2, 1, 3)]
    got["g_z"] = []
    l_wd = load(wd_in, wd)
    l_gate = load(gate_in, gate.at[chip, k])
    l_up = load(up_in, up.at[chip, k])
    l_tok = load(tok_in, tok.at[y, zh])
    l_wg = load(wg_in, wg)
    l_wu = load(wu_in, wu)

    steps = dict(
        u_x=u_x,
        uz=uz,
        g_x=g_x,
        turn_down=turn_down,
        turn_up=turn_up,
        u_relay=u_relay,
        tok_h=tok_h,
        go_y=go_y,
        s0=s0,
        g_relay=g_relay,
        gz12=gz12,
        u_other=u_other,
        gz3=gz3,
        s1=s1,
        s2=s2,
        u_other_relay=u_other_relay,
        gz0=gz0,
        s3=s3,
        tok_y=tok_y,
        s4=s4,
        gather_core=gather_core,
        s5=s5,
        core_arrive=core_arrive,
        s6=s6,
        s7=s7,
        wg=wg_grads,
        final=final,
    )
    for name, *at in SCHEDULE:
        steps[name](*at)
    for c in copies:
        c.wait_send()


def finish(gt, gg, gu, hid, go, gt_out, gg_out, gu_out, gd_out, gd, sem):
    moves = []

    def move(src, dst):
        moves.append(pltpu.make_async_copy(src, dst, sem.at[len(moves)]))
        moves[-1].start()

    for src, dst in ((gg, gg_out), (gu, gu_out)):
        for i in range(2):
            r = pl.ds(i * FEAT // 2, FEAT // 2)
            move(src.at[r], dst.at[r])
    move(gt, gt_out)
    b = go[...].reshape(TOK, FEAT)
    for i in range(7):
        r = pl.ds(i * 256, 256)
        gd[r] = dot(hid[:, :, r].reshape(TOK, 256), b, TN).astype(BF16)
        move(gd.at[r], gd_out.at[r])
    for m in moves:
        m.wait()


def on_device(tokens, gate_pre, up_pre, grad_out, gate_weight, up_weight, down_weight):
    hbm = pl.BlockSpec(memory_space=pl.ANY)
    vmem = pl.BlockSpec(memory_space=pltpu.VMEM)
    bf = lambda *s: pltpu.VMEM(s, BF16)
    fl = lambda *s: pltpu.VMEM(s, F32)
    n = len(ORDER)
    made = pl.pallas_call(
        kernel,
        out_shape=(
            bf(64, FEAT), bf(FEAT, HID), bf(FEAT, HID), bf(4, PLANE, HID), bf(4, 4, 64, FEAT)
        ),
        in_specs=[hbm] * 7,
        out_specs=(vmem,) * 5,
        scratch_shapes=[
            bf(FEAT, HID), bf(FEAT, HID), bf(HID, FEAT),
            bf(HID, FEAT), bf(HID, FEAT), bf(FEAT, HID),
            bf(4, 4, 64, FEAT), bf(4, 4, 64, FEAT),
            bf(8, 2, 64, HID), bf(8, 2, 64, HID),
            bf(4, PLANE, HID), bf(4, PLANE, HID),
            bf(2, 4, PLANE, HALF),
            fl(n, CHUNK, HALF), fl(n, CHUNK, HALF), fl(n, CHUNK, HALF),
            bf(n, CHUNK, HALF), bf(n, 3, PART, HALF),
            fl(n, PART, HALF), bf(n, PART, HALF), bf(n, PART, HALF),
            bf(3, PLANE, FEAT), bf(3, PLANE, FEAT), fl(PLANE, FEAT),
            bf(PLANE, FEAT), bf(3, 64, FEAT),
            pltpu.SemaphoreType.DMA((N_COPY,)),
            pltpu.SemaphoreType.DMA((N_COPY,)),
            pltpu.SemaphoreType.DMA((8,)),
        ],
        compiler_params=pltpu.CompilerParams(
            collective_id=0, has_side_effects=True, vmem_limit_bytes=53 * 2**20
        ),
        cost_estimate=pl.CostEstimate(
            flops=10 * TOK * FEAT * HID, bytes_accessed=2**24, transcendentals=TOK * HID
        ),
        name="swiglu_backward",
    )(tokens, gate_pre, up_pre, grad_out, gate_weight, up_weight, down_weight)
    return pl.pallas_call(
        finish,
        out_shape=tuple(
            jax.ShapeDtypeStruct(shape, BF16)
            for shape in ((64, FEAT), (FEAT, HID), (FEAT, HID), (HID, FEAT))
        ),
        in_specs=[vmem] * 5,
        out_specs=(hbm,) * 4,
        scratch_shapes=[bf(HID, FEAT), pltpu.SemaphoreType.DMA((12,))],
        compiler_params=pltpu.CompilerParams(vmem_limit_bytes=10 * 2**20),
        name="finish",
    )(*(pltpu.with_memory_space_constraint(m, pltpu.VMEM) for m in made))


def solution(mesh):
    in_specs = (
        P("col", "row"),
        P("row", "col"),
        P("row", "col"),
        P("col", "row"),
        P("row", "col"),
        P("row", "col"),
        P("col", "row"),
    )
    out_specs = (P("col", "row"), P("row", "col"), P("row", "col"), P("col", "row"))
    return jax.shard_map(
        on_device, mesh=mesh, in_specs=in_specs, out_specs=out_specs, check_vma=False
    )
```
